256 devices in a mesh: owner: 128 (over z, y, x), ens: 2 (over core).
Axes of the slice: x: 4, y: 4, z: 8, core: 2. Of those that a mesh axis runs over, the one named last changes fastest.
Arguments:
- noisy_state: bfloat16 [4, 12, 8192, 128], P('ens', None, 'owner'), may hold values from -6 to 6
- condition: bfloat16 [12, 8192, 128], P(None, 'owner'), may hold values from -6 to 6
- counts: int32 [128], P('owner'), may hold values from 1 to 4, as said below
- offsets: int32 [128], P('owner'), may hold values from 0 to 64
- conv_in_weight: bfloat16 [3, 3, 24, 128], replicated, may hold values from -0.4375 to 0.4375
- conv_mid_weight: bfloat16 [3, 3, 128, 128], replicated, may hold values from -0.1875 to 0.1875
- proj_out_weight: bfloat16 [12, 128], replicated, may hold values from -0.5 to 0.5
- modulation: float32 [2, 128], replicated, may hold values from -3 to 3
Outputs:
- next_state: float32 [4, 12, 8192, 128], P('ens', None, 'owner')
The draws below stay inside these ranges and needn't reach their ends.
Inputs may be any that keep to these rules, and one draw needn't show every extreme that they name: `counts`: some tile runs all 4 members in every draw.
All inputs are finite; a program needn't handle non-finite values.
Results may differ from the reference program's by a relative error of at most 0.00032.
Values may be sent and summed in bfloat16 or wider, within the bound.
A program may use at most 320 MiB of HBM per device.

```python
import math
import jax
import jax.numpy as jnp
from jax import lax

C = 12
F = 128
GROUPS = 32
BW = 64
H = 128
PW = 128
MMAX = 4
NT = 128
W = 8192


def draw_counts(key, part):
    key = jax.random.fold_in(key, 11)
    centres = jax.random.randint(key, (3,), 0, NT)
    tile_ids = jnp.arange(NT)
    distance = jnp.abs(tile_ids[:, None] - centres[None, :])
    distance = jnp.minimum(distance, NT - distance)
    extra_members = jnp.max(jnp.maximum(MMAX - 1 - distance, 0), axis=1)
    return (1 + extra_members).astype(jnp.int32)


def touch_ends(values, stream_key, low, largest):
    place = [jax.random.randint(jax.random.fold_in(stream_key, axis), (), 0, length) for axis, length in enumerate(values.shape)]
    main_axis = values.shape.index(max(values.shape))
    neighbour = place[:main_axis] + [(place[main_axis] + 1) % values.shape[main_axis]] + place[main_axis + 1:]
    return values.at[tuple(place)].set(low).at[tuple(neighbour)].set(largest)


def block_levels(own_key, dims, cuts, smallest, top_value):
    def one(axis_at, shards_of):
        steps = jax.random.uniform(jax.random.fold_in(jax.random.fold_in(own_key, 6), axis_at), (shards_of,), jnp.float32, smallest / len(cuts), top_value / len(cuts))
        return jnp.repeat(jnp.exp(steps), dims[axis_at] // shards_of).reshape((-1,) + (1,) * (len(dims) - axis_at - 1))

    loudness = one(*cuts[0])
    for cut in cuts[1:]:
        loudness = loudness * one(*cut)
    return loudness


def scatter_about(key, extent, scale, most, shards=(), held_as=jnp.bfloat16):
    entries = jax.random.normal(key, extent, jnp.float32) * scale
    if len(shards) > 0:
        entries = block_levels(key, extent, shards, -0.22, 0.18) * entries
    return jnp.clip(entries, min=-most, max=most).astype(held_as)


def setup_inputs(seed: int = 0) -> dict:
    splits = jax.random.split(jax.random.key(seed), 9)
    noisy_state = scatter_about(splits[0], (MMAX, C, W, H), 1.0, 6.0, ((0, 2), (2, 128)))
    condition = scatter_about(splits[1], (C, W, H), 1.0, 6.0, ((1, 128),))
    counts = draw_counts(jax.random.fold_in(splits[8], 71), 0)
    offsets = touch_ends(jax.random.randint(splits[3], (NT,), 0, BW + 1), jax.random.fold_in(splits[3], 1), 0, BW).astype(jnp.int32)
    conv_in_weight = scatter_about(splits[4], (3, 3, 2 * C, F), (18 * C) ** -0.5, 0.4375)
    conv_mid_weight = scatter_about(splits[5], (3, 3, F, F), (9 * F) ** -0.5, 0.1875)
    proj_out_weight = scatter_about(splits[6], (C, F), F ** -0.5, 0.5)
    modulation = scatter_about(splits[7], (2, F), 0.5, 3.0, (), jnp.float32)
    return dict(noisy_state=noisy_state, condition=condition, counts=counts, offsets=offsets, conv_in_weight=conv_in_weight, conv_mid_weight=conv_mid_weight, proj_out_weight=proj_out_weight, modulation=modulation)


sigma_now = 2.0
sigma_next = 1.0
sigma_data = 0.5
input_scale = 1.0 / math.sqrt(sigma_now ** 2 + sigma_data ** 2)
skip_scale = sigma_data ** 2 / (sigma_now ** 2 + sigma_data ** 2)
output_scale = sigma_now * sigma_data / math.sqrt(sigma_now ** 2 + sigma_data ** 2)
step_factor = (sigma_next - sigma_now) / sigma_now
norm_epsilon = 1e-05

def blend_weights(length_cells):
    places = jnp.arange(length_cells).astype(jnp.float32)
    return 0.1 + jnp.sin(math.pi * (places + 0.5) / length_cells) ** 2

def group_norm(values, groups):
    channels, columns, row_count = values.shape
    grouped = values.reshape(groups, channels // groups, columns, row_count)
    center = lax.optimization_barrier(jnp.mean(grouped, axis=(1, 2, 3), keepdims=True))
    spread = lax.optimization_barrier(jnp.mean(jnp.square(grouped - center), axis=(1, 2, 3), keepdims=True))
    return ((grouped - center) / jnp.sqrt(spread + norm_epsilon)).reshape(channels, columns, row_count)

def convolve(values, kernel):
    columns, row_count = (values.shape[1], values.shape[2])
    padded = jnp.pad(values, ((0, 0), (1, 1), (1, 1)))
    total = jnp.zeros((kernel.shape[3], columns, row_count), jnp.float32)
    for across in range(3):
        for downward in range(3):
            window = padded[:, across:across + columns, downward:downward + row_count]
            total = total + jnp.einsum('cxy,cf->fxy', window, kernel[across, downward].astype(jnp.float32))
    return total

def member_update(noisy_tile, context, conv_in_weight, conv_mid_weight, proj_out_weight, modulation):
    noisy_float = noisy_tile.astype(jnp.float32)
    scaled = lax.optimization_barrier((input_scale * noisy_float).astype(jnp.bfloat16))
    stacked = jnp.concatenate([scaled, context], axis=0).astype(jnp.float32)
    first_conv = convolve(stacked, conv_in_weight)
    modulated = group_norm(first_conv, GROUPS) * (1.0 + modulation[0][:, None, None]) + modulation[1][:, None, None]
    hidden = lax.optimization_barrier(jax.nn.silu(modulated).astype(jnp.bfloat16)).astype(jnp.float32)
    second = convolve(hidden, conv_mid_weight)
    mixed_out = lax.optimization_barrier(jax.nn.silu(group_norm(first_conv + second, GROUPS)).astype(jnp.bfloat16)).astype(jnp.float32)
    output = jnp.einsum('fxy,cf->cxy', mixed_out, proj_out_weight.astype(jnp.float32))
    denoised = skip_scale * noisy_float + output_scale * output
    return step_factor * (noisy_float - denoised)

def reference(noisy_state, condition, counts, offsets, conv_in_weight, conv_mid_weight, proj_out_weight, modulation):
    ext_state = jnp.concatenate([noisy_state[:, :, W - BW:], noisy_state, noisy_state[:, :, :BW]], axis=2)
    ext_cond = jnp.concatenate([condition[:, W - BW:], condition, condition[:, :BW]], axis=1)
    blending = blend_weights(PW)
    member_ids = jnp.arange(MMAX).astype(jnp.int32)

    def one_tile(carried, tile_index):
        numerator, weight_sum = carried
        tile_start = (tile_index * BW + offsets[tile_index]).astype(jnp.int32)
        noisy_tiles = lax.dynamic_slice_in_dim(ext_state, tile_start, PW, 2)
        context = lax.dynamic_slice_in_dim(ext_cond, tile_start, PW, 1)
        tile_count = counts[tile_index]

        def one_member(member_pair):
            update = member_update(member_pair[0], context, conv_in_weight, conv_mid_weight, proj_out_weight, modulation)
            return jnp.where(member_pair[1] < tile_count, blending[None, :, None] * update, 0.0)
        member_terms = lax.map(one_member, (noisy_tiles, member_ids))
        current = lax.dynamic_slice_in_dim(numerator, tile_start, PW, 2)
        numerator = lax.dynamic_update_slice_in_dim(numerator, current + member_terms, tile_start, 2)
        present = lax.dynamic_slice_in_dim(weight_sum, tile_start, PW, 0)
        weight_sum = lax.dynamic_update_slice_in_dim(weight_sum, present + blending, tile_start, 0)
        return ((numerator, weight_sum), None)
    initial = (jnp.zeros((MMAX, C, W + 2 * BW, H), jnp.float32), jnp.zeros((W + 2 * BW,), jnp.float32))
    (numerator, weight_sum), unused = lax.scan(one_tile, initial, jnp.arange(NT).astype(jnp.int32))
    folded = numerator[:, :, BW:W + BW]
    folded = folded.at[:, :, :BW].add(numerator[:, :, W + BW:])
    folded = folded.at[:, :, W - BW:].add(numerator[:, :, :BW])
    weights = weight_sum[BW:W + BW]
    weights = weights.at[:BW].add(weight_sum[W + BW:])
    weights = weights.at[W - BW:].add(weight_sum[:BW])
    return noisy_state.astype(jnp.float32) + folded / weights[None, None, :, None]
```

```python
import functools
import math

import jax
import jax.numpy as jnp
import numpy as np
from jax import lax
from jax.experimental import pallas as pl
from jax.experimental.pallas import tpu as pltpu
from jax.sharding import PartitionSpec as P

MESH = pl.DeviceIdType.MESH

sigma_now = 2.0
sigma_next = 1.0
sigma_data = 0.5
input_scale = 1.0 / math.sqrt(sigma_now**2 + sigma_data**2)
skip_scale = sigma_data**2 / (sigma_now**2 + sigma_data**2)
output_scale = sigma_now * sigma_data / math.sqrt(sigma_now**2 + sigma_data**2)
step_factor = (sigma_next - sigma_now) / sigma_now
norm_epsilon = 1e-05

C = 12
F = 128
BW = 64
PW = 128
H = 128
STRIDE = 200
PAIRS = 8
ROWS = PAIRS * H
CELLS = PW * H
f32, bf16 = jnp.float32, jnp.bfloat16


def group_mean(v):
    lane = lax.broadcasted_iota(jnp.int32, v.shape, 1)
    pair = v + pltpu.roll(v, F - 1, 1)
    four = pair + pltpu.roll(pair, F - 2, 1)
    head = jnp.where(lane % 4 == 0, four, 0.0)
    two = head + pltpu.roll(head, 1, 1)
    return 0.25 * (two + pltpu.roll(two, 2, 1))


def norm_affine(shift, total, squares):
    total = jnp.broadcast_to(jnp.sum(total, axis=0, keepdims=True), (8, F))
    squares = jnp.broadcast_to(jnp.sum(squares, axis=0, keepdims=True), (8, F))
    delta = total / CELLS
    mean = shift + delta
    center = group_mean(mean)
    spread = group_mean((squares / CELLS - delta * delta) + jnp.square(mean - center))
    rstd = 1.0 / jnp.sqrt(spread + norm_epsilon)
    return rstd, -center * rstd


def silu_of_twice(u):
    return u + u * jnp.tanh(u)


def kernel(
    owners,
    offset_ref,
    count_ref,
    noisy_ref,
    cond_ref,
    w_in_ref,
    w_mid_ref,
    w_out_ref,
    mod_ref,
    blend_ref,
    out_ref,
    own_x,
    own_k,
    side_x,
    side_k,
    plane_send,
    plane_side,
    term_send,
    term_side,
    planes_mid,
    term_mid,
    source,
    stacked,
    feats,
    hidden,
    rolled,
    terms,
    w1,
    w2,
    w3,
    local_sem,
    send_sem,
    recv_sem,
):
    me, core = lax.axis_index("owner"), lax.axis_index("ens")
    left = lax.rem(me + owners - 1, owners)
    right = lax.rem(me + 1, owners)
    targets = (right, left)

    barrier = pltpu.get_barrier_semaphore()
    for neighbour in (left, right):
        pl.semaphore_signal(barrier, inc=1, device_id=(neighbour, core), device_id_type=MESH)

    local = [
        pltpu.make_async_copy(noisy_ref, own_x, local_sem.at[0]),
        pltpu.make_async_copy(cond_ref, own_k, local_sem.at[1]),
        pltpu.make_async_copy(w_mid_ref, rolled.at[pl.ds(0, 9)], local_sem.at[2]),
    ]
    for copy in local:
        copy.start()

    def remote(kind, side, source_ref, target_ref):
        return pltpu.make_async_remote_copy(
            src_ref=source_ref,
            dst_ref=target_ref,
            send_sem=send_sem.at[kind, side],
            recv_sem=recv_sem.at[kind, side],
            device_id=(targets[side], core),
            device_id_type=MESH,
        )

    def both(kind, make):
        return [remote(kind, side, *make(side)) for side in range(2)]

    send_x = [
        both(m, lambda side: (noisy_ref.at[m], side_x.at[side, m])) for m in range(2)
    ]
    send_k = both(2, lambda side: (cond_ref, side_k.at[side]))
    send_plane = both(3, lambda side: (plane_send.at[side], plane_side.at[side]))
    send_term = [
        both(4 + m, lambda side: (term_send.at[side, m], term_side.at[side, m]))
        for m in range(2)
    ]

    pl.semaphore_wait(barrier, 2)
    for copy in send_x[0] + send_k:
        copy.start()

    offset, count = offset_ref[0], count_ref[0]
    active = [core * 2 + m < count for m in range(2)]

    terms[0, pl.ds(0, BW)] = jnp.zeros((BW, H), f32)
    terms[0, pl.ds(BW, PW)] = blend_ref[...]
    terms[0, pl.ds(BW + PW, BW)] = jnp.zeros((BW, H), f32)
    for block, target in ((0, plane_send.at[1]), (1, planes_mid), (2, plane_send.at[0])):
        plane = terms[0, pl.ds(BW + BW * block - offset, BW)]
        target[0] = plane
        for m in range(2):
            target[1 + m] = jnp.where(active[m], plane, 0.0)
    for copy in send_plane:
        copy.start()
    terms[:, pl.ds(0, BW)] = jnp.zeros((C, BW, H), f32)
    terms[:, pl.ds(BW + PW, BW)] = jnp.zeros((C, BW, H), f32)

    taps = w_in_ref[...].astype(f32)
    zeros8, zeros32 = jnp.zeros((8, F), f32), jnp.zeros((32, F), f32)
    zeros128 = jnp.zeros((F, F), bf16)
    for ci in range(4):
        for p in range(2):
            a = ci - p
            if 0 <= a < 3:
                pieces = []
                for b in range(3):
                    pieces += [taps[(a * 3 + b) * 24 : (a * 3 + b) * 24 + 24], zeros8]
                block = jnp.concatenate(pieces + [zeros32], axis=0).astype(bf16)
            else:
                block = zeros128
            w1[pl.ds(ci * 128, 128), pl.ds(p * 128, 128)] = block
    out_rows = jnp.concatenate([w_out_ref[...].astype(f32), jnp.zeros((4, F), f32)], axis=0)
    spread_rows = jnp.broadcast_to(out_rows[:, None, :], (16, 8, F)).reshape(F, F).T
    lane = lax.broadcasted_iota(jnp.int32, (F, F), 1)
    for k in range(8):
        w3[pl.ds(k * 128, 128)] = jnp.where(lane % 8 == k, spread_rows, 0.0).astype(bf16)
    local[2].wait()
    for b in range(3):
        for ci in range(4):
            for p in range(2):
                a = ci - p
                block = rolled[a * 3 + b] if 0 <= a < 3 else zeros128
                w2[pl.ds((b * 4 + ci) * 128, 128), pl.ds(p * 128, 128)] = block

    for ref in (stacked,):
        ref[0, 0] = zeros128
        ref[1, BW] = zeros128
    for b in range(3):
        hidden[b, 0, 0] = zeros128
        hidden[b, 1, BW] = zeros128

    def put_state(ref, block):
        for c in range(C):
            scaled = (input_scale * ref[c].astype(f32)).astype(bf16).astype(f32)
            source[pl.ds(c * STRIDE + block * BW, BW)] = scaled

    def put_cond(ref, block):
        for c in range(C):
            source[pl.ds((C + c) * STRIDE + block * BW, BW)] = ref[c].astype(f32)

    local[0].wait()
    local[1].wait()
    put_cond(own_k, 1)
    for copy in send_k:
        copy.wait_recv()
    put_cond(side_k.at[0], 0)
    put_cond(side_k.at[1], 2)

    def stack_column(column):
        v = source[pl.ds(offset + column, 24, stride=STRIDE), :]
        row = lax.broadcasted_iota(jnp.int32, v.shape, 1)
        before = jnp.where(row == 0, 0.0, pltpu.roll(v, 1, 1))
        after = jnp.where(row == H - 1, 0.0, pltpu.roll(v, H - 1, 1))
        full = jnp.concatenate([before, zeros8, v, zeros8, after, zeros8, zeros32], axis=0)
        return full.T.astype(bf16)

    def stack_step(i, carry):
        for s in range(8):
            slot = i * 8 + s
            stacked[1, slot] = stack_column(2 * slot)
            stacked[0, slot + 1] = stack_column(2 * slot + 1)
        return carry

    def gather(refs, step):
        columns = []
        for ref in refs:
            for ci in range(4):
                part = ref[ci % 2, pl.ds(step * PAIRS + ci // 2, PAIRS)]
                columns.append(part.reshape(ROWS, F))
        return jnp.concatenate(columns, axis=1)

    def conv_step(step, carry, refs, w, add):
        shift, total, squares = carry
        acc = jnp.dot(gather(refs, step), w[...], preferred_element_type=f32)
        halves = []
        for p in range(2):
            half = acc[:, p * F : (p + 1) * F].reshape(PAIRS, H, F)
            if add:
                half = half + feats[p, pl.ds(step * PAIRS, PAIRS)]
            feats[p, pl.ds(step * PAIRS, PAIRS)] = half
            halves.append(half.reshape(ROWS // 8, 8, F))
        if shift is None:
            shift = (jnp.sum(halves[0], axis=0) + jnp.sum(halves[1], axis=0)) / (2 * ROWS // 8)
            shift = jnp.broadcast_to(jnp.mean(shift, axis=0, keepdims=True), (8, F))
        for half in halves:
            deviation = half - shift
            total = total + jnp.sum(deviation, axis=0)
            squares = squares + jnp.sum(deviation * deviation, axis=0)
        return shift, total, squares

    def conv(refs, w, add):
        zero = jnp.zeros((8, F), f32)
        carry = conv_step(0, (None, zero, zero), refs, w, add)
        step = functools.partial(conv_step, refs=refs, w=w, add=add)
        return lax.fori_loop(1, BW // PAIRS, step, carry)

    def hidden_step(i, carry):
        scale, bias = carry
        for s in range(4):
            slot = i * 4 + s
            for p in range(2):
                h = silu_of_twice(feats[p, slot] * scale + bias)
                row = lax.broadcasted_iota(jnp.int32, h.shape, 0)
                before = jnp.where(row == 0, 0.0, pltpu.roll(h, 1, 0))
                after = jnp.where(row == H - 1, 0.0, pltpu.roll(h, H - 1, 0))
                for b, value in enumerate((before, h, after)):
                    hidden[b, 1 - p, slot + p] = value.astype(bf16)
        return carry

    def out_step(i, carry):
        scale, bias = carry
        columns = []
        for k in range(8):
            rows = []
            for g in range(4):
                u = feats[k % 2, i * 16 + g * 4 + k // 2] * scale + bias
                rows.append(silu_of_twice(u).astype(bf16))
            columns.append(jnp.concatenate(rows, axis=0))
        result = jnp.dot(
            jnp.concatenate(columns, axis=1), w3[...], preferred_element_type=f32
        )
        for g in range(4):
            flipped = result[g * H : (g + 1) * H].T.reshape(16, 8, H)[:C]
            weight = blend_ref[pl.ds(i * 32 + g * 8, 8)] * (-step_factor * output_scale)
            terms[:, pl.ds(BW + i * 32 + g * 8, 8)] = flipped * weight
        return carry

    for m in range(2):
        put_state(own_x.at[m], 1)
        for copy in send_x[m]:
            copy.wait_recv()
        if m == 0:
            for copy in send_x[1]:
                copy.start()
        put_state(side_x.at[0, m], 0)
        put_state(side_x.at[1, m], 2)
        lax.fori_loop(0, 8, stack_step, 0)
        scale, bias = norm_affine(*conv((stacked,), w1, False))
        gain = 1.0 + mod_ref[0:1]
        scale, bias = scale * gain * 0.5, (bias * gain + mod_ref[1:2]) * 0.5
        lax.fori_loop(0, 16, hidden_step, (scale[0:1], bias[0:1]))
        scale, bias = norm_affine(*conv([hidden.at[b] for b in range(3)], w2, True))
        lax.fori_loop(0, 4, out_step, (scale[0:1] * 0.5, bias[0:1] * 0.5))
        for block, target in (
            (0, term_send.at[1, m]),
            (2, term_send.at[0, m]),
            (1, term_mid.at[m]),
        ):
            for c in range(C):
                part = terms[c, pl.ds(BW + BW * block - offset, BW)]
                target[c] = jnp.where(active[m], part, 0.0)
            if block == 2:
                for copy in send_term[m]:
                    copy.start()

    for copy in send_plane:
        copy.wait_recv()
    planes = [planes_mid[q] + plane_side[0, q] + plane_side[1, q] for q in range(3)]
    inverse = 1.0 / planes[0]
    for m in range(2):
        for copy in send_term[m]:
            copy.wait_recv()
        factor = planes[1 + m] * (step_factor * (1.0 - skip_scale))
        for c in range(C):
            x = own_x[m, c].astype(f32)
            numerator = term_mid[m, c] + term_side[0, m, c] + term_side[1, m, c]
            out_ref[m, c] = x + (x * factor + numerator) * inverse

    for copy in send_x[0] + send_x[1] + send_k + send_plane + send_term[0] + send_term[1]:
        copy.wait_send()


def solution(mesh):
    owners = mesh.shape["owner"]
    places = (np.arange(PW) + 0.5).astype(np.float32)
    blend = 0.1 + np.sin(np.float32(math.pi) * places / np.float32(PW)) ** 2
    blend = np.broadcast_to(blend.astype(np.float32)[:, None], (PW, H))

    def on_device(noisy, cond, counts, offsets, w_in, w_mid, w_out, mod):
        smem = pl.BlockSpec(memory_space=pltpu.SMEM)
        vmem = pl.BlockSpec(memory_space=pltpu.VMEM)
        hbm = pl.BlockSpec(memory_space=pl.ANY)
        return pl.pallas_call(
            functools.partial(kernel, owners),
            out_shape=jax.ShapeDtypeStruct((2, C, BW, H), f32),
            in_specs=[smem, smem, hbm, hbm, vmem, hbm, vmem, vmem, vmem],
            out_specs=vmem,
            scratch_shapes=[
                pltpu.VMEM((2, C, BW, H), bf16),
                pltpu.VMEM((C, BW, H), bf16),
                pltpu.VMEM((2, 2, C, BW, H), bf16),
                pltpu.VMEM((2, C, BW, H), bf16),
                pltpu.VMEM((2, 3, BW, H), f32),
                pltpu.VMEM((2, 3, BW, H), f32),
                pltpu.VMEM((2, 2, C, BW, H), f32),
                pltpu.VMEM((2, 2, C, BW, H), f32),
                pltpu.VMEM((3, BW, H), f32),
                pltpu.VMEM((2, C, BW, H), f32),
                pltpu.VMEM((2 * C * STRIDE, H), f32),
                pltpu.VMEM((2, BW + 1, H, F), bf16),
                pltpu.VMEM((2, BW, H, F), f32),
                pltpu.VMEM((3, 2, BW + 1, H, F), bf16),
                pltpu.VMEM((9, F, F), bf16),
                pltpu.VMEM((C, 2 * PW, H), f32),
                pltpu.VMEM((4 * F, 2 * F), bf16),
                pltpu.VMEM((12 * F, 2 * F), bf16),
                pltpu.VMEM((8 * F, F), bf16),
                pltpu.SemaphoreType.DMA((3,)),
                pltpu.SemaphoreType.DMA((6, 2)),
                pltpu.SemaphoreType.DMA((6, 2)),
            ],
            compiler_params=pltpu.CompilerParams(
                collective_id=0, has_side_effects=True, vmem_limit_bytes=56 * 2**20
            ),
            cost_estimate=pl.CostEstimate(
                flops=24 * 10**9, bytes_accessed=4 * 10**6, transcendentals=8 * 10**6
            ),
        )(
            offsets,
            counts,
            noisy,
            cond,
            w_in.reshape(216, F),
            w_mid.reshape(9, F, F),
            w_out,
            mod,
            jnp.asarray(blend),
        )

    placed = (
        P("ens", None, "owner", None),
        P(None, "owner", None),
        P("owner"),
        P("owner"),
        P(),
        P(),
        P(),
        P(),
    )
    return jax.shard_map(
        on_device,
        mesh=mesh,
        in_specs=placed,
        out_specs=P("ens", None, "owner", None),
        check_vma=False,
    )
```

```python
import functools
import math

import jax
import jax.numpy as jnp
import numpy as np
from jax import lax
from jax.experimental import pallas as pl
from jax.experimental.pallas import tpu as pltpu
from jax.sharding import PartitionSpec as P

MESH = pl.DeviceIdType.MESH

sigma_now = 2.0
sigma_next = 1.0
sigma_data = 0.5
input_scale = 1.0 / math.sqrt(sigma_now**2 + sigma_data**2)
skip_scale = sigma_data**2 / (sigma_now**2 + sigma_data**2)
output_scale = sigma_now * sigma_data / math.sqrt(sigma_now**2 + sigma_data**2)
step_factor = (sigma_next - sigma_now) / sigma_now
norm_epsilon = 1e-05

C = 12
F = 128
BW = 64
PW = 128
H = 128
STRIDE = 200
LANES = 40
PAIRS = 8
OWN = 30
OWN_STEP = 10
REST_STEP = 12
CELLS = PW * H
LEVELS = 32767.0
f32, bf16 = jnp.float32, jnp.bfloat16


def group_mean(v):
    lane = lax.broadcasted_iota(jnp.int32, v.shape, 1)
    pair = v + pltpu.roll(v, F - 1, 1)
    four = pair + pltpu.roll(pair, F - 2, 1)
    head = jnp.where(lane % 4 == 0, four, 0.0)
    two = head + pltpu.roll(head, 1, 1)
    return 0.25 * (two + pltpu.roll(two, 2, 1))


def merge(stats, count, total, squares):
    number, mean, spread = stats
    total = jnp.broadcast_to(jnp.sum(total, axis=0, keepdims=True), (8, F))
    squares = jnp.broadcast_to(jnp.sum(squares, axis=0, keepdims=True), (8, F))
    number = number + count
    return number, mean + total / number, spread + (squares - total * total / number)


def norm_affine(mean, squares):
    center = group_mean(mean)
    spread = group_mean(squares / CELLS + jnp.square(mean - center))
    rstd = 1.0 / jnp.sqrt(spread + norm_epsilon)
    return rstd, -center * rstd


def silu_of_twice(u):
    return u + u * jnp.tanh(u)


def kernel(
    owners,
    offset_ref,
    count_ref,
    noisy_ref,
    cond_ref,
    w_in_ref,
    w_mid_ref,
    w_out_ref,
    mod_ref,
    blend_ref,
    out_ref,
    own_x,
    own_k,
    side_x,
    side_k,
    plane_send,
    plane_side,
    term_send,
    term_side,
    step_send,
    step_side,
    planes_mid,
    term_mid,
    source,
    stacked,
    ring1,
    ring1b,
    feats,
    sums,
    ring2,
    ring2b,
    rolled,
    terms,
    w1,
    w1b,
    w2,
    w3,
    local_sem,
    send_sem,
    recv_sem,
):
    me, core = lax.axis_index("owner"), lax.axis_index("ens")
    left = lax.rem(me + owners - 1, owners)
    right = lax.rem(me + 1, owners)
    targets = (right, left)

    barrier = pltpu.get_barrier_semaphore()
    for neighbour in (left, right):
        pl.semaphore_signal(barrier, inc=1, device_id=(neighbour, core), device_id_type=MESH)

    local = [
        pltpu.make_async_copy(noisy_ref, own_x, local_sem.at[0]),
        pltpu.make_async_copy(cond_ref, own_k, local_sem.at[1]),
        pltpu.make_async_copy(w_mid_ref, rolled, local_sem.at[2]),
    ]
    for copy in local:
        copy.start()

    def both(kind, make):
        copies = []
        for side in range(2):
            source_ref, target_ref = make(side)
            copies.append(
                pltpu.make_async_remote_copy(
                    src_ref=source_ref,
                    dst_ref=target_ref,
                    send_sem=send_sem.at[kind, side],
                    recv_sem=recv_sem.at[kind, side],
                    device_id=(targets[side], core),
                    device_id_type=MESH,
                )
            )
        return copies

    send_x = [
        both(m, lambda side: (noisy_ref.at[m], side_x.at[side, m])) for m in range(2)
    ]
    send_k = both(2, lambda side: (cond_ref, side_k.at[side]))
    send_plane = both(3, lambda side: (plane_send.at[side], plane_side.at[side]))
    send_term = [
        both(4 + m, lambda side: (term_send.at[side, m], term_side.at[side, m]))
        for m in range(2)
    ]
    send_step = [
        both(6 + m, lambda side: (step_send.at[side, m], step_side.at[side, m]))
        for m in range(2)
    ]

    pl.semaphore_wait(barrier, 2)
    for copy in send_x[0] + send_k:
        copy.start()

    offset, count = offset_ref[0], count_ref[0]
    active = [core * 2 + m < count for m in range(2)]
    odd = offset & 1
    even = offset - odd
    left_pairs = 33 - (offset >> 1)

    taps = w_in_ref[...].astype(f32)
    zeros128 = jnp.zeros((F, F), bf16)
    zeros8, zeros16 = jnp.zeros((8, F), f32), jnp.zeros((16, F), f32)
    for ci in range(4):
        for p in range(2):
            a = ci - p
            block = block_b = zeros128
            if 0 <= a < 3:
                pieces, pieces_b = [], []
                for b in range(3):
                    tap = taps[(a * 3 + b) * 24 : (a * 3 + b) * 24 + 24]
                    pieces += [tap, zeros16]
                    pieces_b += [zeros16[:C], tap[C:], tap[:C], zeros16[:4]]
                block = jnp.concatenate(pieces + [zeros8], axis=0).astype(bf16)
                block_b = jnp.concatenate(pieces_b + [zeros8], axis=0).astype(bf16)
            w1[pl.ds(ci * 128, 128), pl.ds(p * 128, 128)] = block
            w1b[pl.ds(ci * 128, 128), pl.ds(p * 128, 128)] = block_b

    def put_state(ref, slot, block):
        for c in range(C):
            scaled = (input_scale * ref[c].astype(f32)).astype(bf16).astype(f32)
            source[pl.ds((slot + c) * STRIDE + block * BW, BW)] = scaled

    def put_cond(ref, block):
        for c in range(C):
            source[pl.ds((C + c) * STRIDE + block * BW, BW)] = ref[c].astype(f32)

    local[0].wait()
    local[1].wait()
    source[pl.ds(36 * STRIDE, 4 * STRIDE)] = jnp.zeros((4 * STRIDE, H), f32)
    put_cond(own_k, 1)
    put_state(own_x.at[0], 0, 1)
    put_state(own_x.at[1], 24, 1)

    def stack_column(column, channels, valid=None):
        v = source[pl.ds(column, channels, stride=STRIDE), :]
        if valid is not None:
            v = jnp.where(valid, v, 0.0)
        row = lax.broadcasted_iota(jnp.int32, v.shape, 1)
        before = jnp.where(row == 0, 0.0, pltpu.roll(v, 1, 1))
        after = jnp.where(row == H - 1, 0.0, pltpu.roll(v, H - 1, 1))
        pieces = []
        for part in (before, v, after):
            pieces += [part] if channels == LANES else [part, zeros16]
        return jnp.concatenate(pieces + [zeros8], axis=0).T.astype(bf16)

    def own_stack_step(i, carry):
        for t in range(16):
            stacked[t % 2, i * 8 + t // 2] = stack_column(BW + 1 + i * 16 + t, LANES)
        return carry

    lax.fori_loop(0, 4, own_stack_step, 0)

    def deviations(stats, values, keep=None):
        deviation = values.reshape(-1, 8, F) - stats[1]
        if keep is not None:
            deviation = jnp.where(keep, deviation, 0.0)
        return jnp.sum(deviation, axis=0), jnp.sum(deviation * deviation, axis=0)

    def own_conv(m):
        def step(i, stats):
            columns = []
            for ci in range(4):
                part = stacked[ci % 2, pl.ds(i * OWN_STEP + ci // 2, OWN_STEP)]
                columns.append(part.reshape(OWN_STEP * H, F))
            lhs = jnp.concatenate(columns, axis=1)
            acc = jnp.dot(lhs, (w1, w1b)[m][...], preferred_element_type=f32)
            total = squares = jnp.zeros((8, F), f32)
            for p in range(2):
                half = acc[:, p * F : (p + 1) * F]
                feats[p, pl.ds(m * OWN + i * OWN_STEP, OWN_STEP)] = half.reshape(
                    OWN_STEP, H, F
                )
                more = deviations(stats, half)
                total, squares = total + more[0], squares + more[1]
            return merge(stats, 2.0 * OWN_STEP * H, total, squares)

        zero = jnp.zeros((8, F), f32)
        return lax.fori_loop(0, OWN // OWN_STEP, step, (zero, zero, zero))

    own_stats = [own_conv(m) for m in range(2)]

    terms[0, pl.ds(0, BW)] = jnp.zeros((BW, H), f32)
    terms[0, pl.ds(BW, PW)] = blend_ref[...]
    terms[0, pl.ds(BW + PW, BW)] = jnp.zeros((BW, H), f32)
    for block, target in ((0, plane_send.at[1]), (1, planes_mid), (2, plane_send.at[0])):
        plane = terms[0, pl.ds(BW + BW * block - offset, BW)]
        target[0] = plane
        for m in range(2):
            target[1 + m] = jnp.where(active[m], plane, 0.0)
    for copy in send_plane:
        copy.start()
    terms[:, pl.ds(0, BW)] = jnp.zeros((C, BW, H), f32)
    terms[:, pl.ds(BW + PW, BW)] = jnp.zeros((C, BW, H), f32)

    out_rows = jnp.concatenate([w_out_ref[...].astype(f32), jnp.zeros((4, F), f32)], axis=0)
    spread_rows = jnp.broadcast_to(out_rows[:, None, :], (16, 8, F)).reshape(F, F).T
    lane = lax.broadcasted_iota(jnp.int32, (F, F), 1)
    for k in range(8):
        w3[pl.ds(k * 128, 128)] = jnp.where(lane % 8 == k, spread_rows, 0.0).astype(bf16)
    local[2].wait()
    for b in range(3):
        for ci in range(4):
            for p in range(2):
                a = ci - p
                block = rolled[a * 3 + b] if 0 <= a < 3 else zeros128
                w2[pl.ds((b * 4 + ci) * 128, 128), pl.ds(p * 128, 128)] = block

    rings1, rings2 = (ring1, ring1b), (ring2, ring2b)

    def rest_stack(g):
        for t in range(2 * REST_STEP + 4):
            place = 2 * REST_STEP * g + t
            first_right = 68 - even
            column = jnp.where(place < first_right, even - 1 + place, 125 - first_right + place)
            valid = (column >= offset) & (column < offset + PW)
            column = jnp.clip(column, 0, STRIDE - 1)
            rings1[g % 2][t % 2, t // 2] = stack_column(column, 24, valid)

    def rest_conv(g, m, stats):
        columns = []
        for ci in range(4):
            parts = []
            for p in range(REST_STEP):
                skip = (REST_STEP * g + p >= left_pairs).astype(jnp.int32)
                parts.append(rings1[g % 2][ci % 2, p + ci // 2 + skip])
            columns.append(jnp.concatenate(parts, axis=0))
        lhs = jnp.concatenate(columns, axis=1)
        acc = jnp.dot(lhs, w1[...], preferred_element_type=f32)
        total = squares = jnp.zeros((8, F), f32)
        number = 2.0 * REST_STEP * H
        for p in range(2):
            half = acc[:, p * F : (p + 1) * F]
            feats[p, pl.ds(2 * OWN + g * REST_STEP, REST_STEP)] = half.reshape(REST_STEP, H, F)
            start, stop = 0, REST_STEP * H
            if g == 0 and p == 0:
                start = H
                more = deviations(stats, half[:H], odd == 0)
                total, squares = total + more[0], squares + more[1]
                number = number - odd.astype(f32) * H
            if g == 2:
                stop = (REST_STEP - 2) * H
                if p == 0:
                    more = deviations(stats, half[stop : stop + H], odd == 1)
                    total, squares = total + more[0], squares + more[1]
                    number = number - 4.0 * H + odd.astype(f32) * H
            more = deviations(stats, half[start:stop])
            total, squares = total + more[0], squares + more[1]
        return merge(stats, number, total, squares)

    def first_at(m, column):
        place = offset + column
        pair, parity = place >> 1, place & 1
        rest = 2 * OWN + jnp.where(pair < 33, pair - (offset >> 1), pair - 63 + left_pairs)
        own = m * OWN + pair - 33
        slot = jnp.where((pair >= 33) & (pair < 63), own, rest)
        return feats[parity, slot]

    def put_hidden(m, affine, column, places):
        h = silu_of_twice(first_at(m, jnp.minimum(column, PW - 1)) * affine[0] + affine[1])
        if any(t == 2 * PAIRS + 1 for _, t in places):
            h = jnp.where(column < PW, h, 0.0)
        row = lax.broadcasted_iota(jnp.int32, h.shape, 0)
        before = jnp.where(row == 0, 0.0, pltpu.roll(h, 1, 0))
        after = jnp.where(row == H - 1, 0.0, pltpu.roll(h, H - 1, 0))
        for b, value in enumerate((before, h, after)):
            for ref, t in places:
                ref[b, t % 2, t // 2] = value.astype(bf16)

    def fill(m, affine, g, here, there):
        for r in range(2 * PAIRS):
            places = [(here, r + 2)]
            if r >= 2 * PAIRS - 2:
                places.append((there, r + 2 - 2 * PAIRS))
            put_hidden(m, affine, 2 * PAIRS * g + 1 + r, places)

    def mid_conv(m, g, ref, stats):
        columns = []
        for b in range(3):
            for ci in range(4):
                part = ref[b, ci % 2, pl.ds(ci // 2, PAIRS)]
                columns.append(part.reshape(PAIRS * H, F))
        acc = jnp.dot(jnp.concatenate(columns, axis=1), w2[...], preferred_element_type=f32)
        total = squares = jnp.zeros((8, F), f32)
        for q in range(PAIRS):
            for p in range(2):
                both_convs = acc[q * H : (q + 1) * H, p * F : (p + 1) * F]
                both_convs = both_convs + first_at(m, 2 * (PAIRS * g + q) + p)
                sums[p, PAIRS * g + q] = both_convs
                more = deviations(stats, both_convs)
                total, squares = total + more[0], squares + more[1]
        return merge(stats, 2.0 * PAIRS * H, total, squares)

    def mid_step(i, carry, m):
        stats, affine = carry
        stats = mid_conv(m, 2 * i, ring2, stats)
        fill(m, affine, 2 * i + 1, ring2b, ring2)
        stats = mid_conv(m, 2 * i + 1, ring2b, stats)
        fill(m, affine, 2 * i + 2, ring2, ring2b)
        return stats, affine

    def out_step(i, carry):
        scale, bias = carry
        for sub in range(2):
            base = i * 32 + sub * 16
            columns = []
            for k in range(8):
                rows = []
                for g in range(4):
                    u = sums[k % 2, base + g * 4 + k // 2] * scale + bias
                    rows.append(silu_of_twice(u).astype(bf16))
                columns.append(jnp.concatenate(rows, axis=0))
            result = jnp.dot(
                jnp.concatenate(columns, axis=1), w3[...], preferred_element_type=f32
            )
            for g in range(4):
                flipped = result[g * H : (g + 1) * H].T.reshape(16, 8, H)[:C]
                at = 2 * base + g * 8
                weight = blend_ref[pl.ds(at, 8)] * (-step_factor * output_scale)
                terms[:, pl.ds(BW + at, 8)] = flipped * weight
        return carry

    for copy in send_k:
        copy.wait_recv()
    put_cond(side_k.at[0], 0)
    put_cond(side_k.at[1], 2)

    for m in range(2):
        if m == 1:
            put_state(own_x.at[m], 0, 1)
        for copy in send_x[m]:
            copy.wait_recv()
        if m == 0:
            for copy in send_x[1]:
                copy.start()
        put_state(side_x.at[0, m], 0, 0)
        put_state(side_x.at[1, m], 0, 2)
        stats = own_stats[m]
        rest_stack(0)
        for g in range(3):
            if g < 2:
                rest_stack(g + 1)
            stats = rest_conv(g, m, stats)
        scale, bias = norm_affine(stats[1], stats[2])
        gain = 1.0 + mod_ref[0:1]
        scale, bias = scale * gain * 0.5, (bias * gain + mod_ref[1:2]) * 0.5
        affine = scale[0:1], bias[0:1]
        for b in range(3):
            ring2[b, 0, 0] = zeros128
        put_hidden(m, affine, jnp.int32(0), [(ring2, 1)])
        fill(m, affine, 0, ring2, ring2b)
        zero = jnp.zeros((8, F), f32)
        (stats, _) = lax.fori_loop(
            0,
            BW // PAIRS // 2,
            functools.partial(mid_step, m=m),
            ((zero, stats[1], zero), affine),
        )
        scale, bias = norm_affine(stats[1], stats[2])
        lax.fori_loop(0, 2, out_step, (scale[0:1] * 0.5, bias[0:1] * 0.5))
        for block, side in ((0, 1), (2, 0)):
            largest = jnp.full((8, H), 1e-30, f32)
            for c in range(C):
                part = terms[c, pl.ds(BW + BW * block - offset, BW)]
                part = jnp.max(jnp.abs(part).reshape(8, 8, H), axis=0)
                largest = jnp.maximum(largest, part)
            step_send[side, m] = jnp.where(active[m], largest * (1.0 / LEVELS), 0.0)
            inverse = LEVELS / largest
            for c in range(C):
                part = terms[c, pl.ds(BW + BW * block - offset, BW)].reshape(8, 8, H)
                levels = jnp.round(part * inverse).astype(jnp.int32)
                term_send[side, m, c] = levels.reshape(BW, H).astype(jnp.int16)
            send_term[m][side].start()
            send_step[m][side].start()
        for c in range(C):
            part = terms[c, pl.ds(2 * BW - offset, BW)]
            term_mid[m, c] = jnp.where(active[m], part, 0.0)

    for copy in send_plane:
        copy.wait_recv()
    planes = [planes_mid[q] + plane_side[0, q] + plane_side[1, q] for q in range(3)]
    inverse = 1.0 / planes[0]
    for m in range(2):
        for copy in send_step[m] + send_term[m]:
            copy.wait_recv()
        factor = planes[1 + m] * (step_factor * (1.0 - skip_scale))
        steps = [step_side[side, m] for side in range(2)]
        for c in range(C):
            x = own_x[m, c].astype(f32)
            numerator = term_mid[m, c]
            for side in range(2):
                levels = term_side[side, m, c].astype(jnp.int32).astype(f32)
                numerator = numerator + (levels.reshape(8, 8, H) * steps[side]).reshape(BW, H)
            out_ref[m, c] = x + (x * factor + numerator) * inverse

    sent = send_k + send_plane
    for m in range(2):
        sent = sent + send_x[m] + send_term[m] + send_step[m]
    for copy in sent:
        copy.wait_send()


def solution(mesh):
    owners = mesh.shape["owner"]
    places = (np.arange(PW) + 0.5).astype(np.float32)
    blend = 0.1 + np.sin(np.float32(math.pi) * places / np.float32(PW)) ** 2
    blend = np.broadcast_to(blend.astype(np.float32)[:, None], (PW, H))

    def on_device(noisy, cond, counts, offsets, w_in, w_mid, w_out, mod):
        smem = pl.BlockSpec(memory_space=pltpu.SMEM)
        vmem = pl.BlockSpec(memory_space=pltpu.VMEM)
        hbm = pl.BlockSpec(memory_space=pl.ANY)
        return pl.pallas_call(
            functools.partial(kernel, owners),
            out_shape=jax.ShapeDtypeStruct((2, C, BW, H), f32),
            in_specs=[smem, smem, hbm, hbm, vmem, hbm, vmem, vmem, vmem],
            out_specs=vmem,
            scratch_shapes=[
                pltpu.VMEM((2, C, BW, H), bf16),
                pltpu.VMEM((C, BW, H), bf16),
                pltpu.VMEM((2, 2, C, BW, H), bf16),
                pltpu.VMEM((2, C, BW, H), bf16),
                pltpu.VMEM((2, 3, BW, H), f32),
                pltpu.VMEM((2, 3, BW, H), f32),
                pltpu.VMEM((2, 2, C, BW, H), jnp.int16),
                pltpu.VMEM((2, 2, C, BW, H), jnp.int16),
                pltpu.VMEM((2, 2, 8, H), f32),
                pltpu.VMEM((2, 2, 8, H), f32),
                pltpu.VMEM((3, BW, H), f32),
                pltpu.VMEM((2, C, BW, H), f32),
                pltpu.VMEM((LANES * STRIDE, H), f32),
                pltpu.VMEM((2, BW // 2, H, F), bf16),
                pltpu.VMEM((2, REST_STEP + 2, H, F), bf16),
                pltpu.VMEM((2, REST_STEP + 2, H, F), bf16),
                pltpu.VMEM((2, 2 * OWN + 3 * REST_STEP, H, F), f32),
                pltpu.VMEM((2, BW, H, F), f32),
                pltpu.VMEM((3, 2, PAIRS + 1, H, F), bf16),
                pltpu.VMEM((3, 2, PAIRS + 1, H, F), bf16),
                pltpu.VMEM((9, F, F), bf16),
                pltpu.VMEM((C, 2 * PW, H), f32),
                pltpu.VMEM((4 * F, 2 * F), bf16),
                pltpu.VMEM((4 * F, 2 * F), bf16),
                pltpu.VMEM((12 * F, 2 * F), bf16),
                pltpu.VMEM((8 * F, F), bf16),
                pltpu.SemaphoreType.DMA((3,)),
                pltpu.SemaphoreType.DMA((8, 2)),
                pltpu.SemaphoreType.DMA((8, 2)),
            ],
            compiler_params=pltpu.CompilerParams(
                collective_id=0, has_side_effects=True, vmem_limit_bytes=56 * 2**20
            ),
            cost_estimate=pl.CostEstimate(
                flops=24 * 10**9, bytes_accessed=4 * 10**6, transcendentals=8 * 10**6
            ),
        )(
            offsets,
            counts,
            noisy,
            cond,
            w_in.reshape(216, F),
            w_mid.reshape(9, F, F),
            w_out,
            mod,
            jnp.asarray(blend),
        )

    placed = (
        P("ens", None, "owner", None),
        P(None, "owner", None),
        P("owner"),
        P("owner"),
        P(),
        P(),
        P(),
        P(),
    )
    return jax.shard_map(
        on_device,
        mesh=mesh,
        in_specs=placed,
        out_specs=P("ens", None, "owner", None),
        check_vma=False,
    )
```

```python
import functools
import math

import jax
import jax.numpy as jnp
from jax import lax
from jax.experimental import pallas as pl
from jax.experimental.pallas import tpu as pltpu
from jax.sharding import PartitionSpec as P

MESH = pl.DeviceIdType.MESH

sigma_now = 2.0
sigma_next = 1.0
sigma_data = 0.5
input_scale = 1.0 / math.sqrt(sigma_now**2 + sigma_data**2)
skip_scale = sigma_data**2 / (sigma_now**2 + sigma_data**2)
output_scale = sigma_now * sigma_data / math.sqrt(sigma_now**2 + sigma_data**2)
step_factor = (sigma_next - sigma_now) / sigma_now
norm_epsilon = 1e-05

C = 12
F = 128
BW = 64
PW = 128
H = 128
STRIDE = 200
LANES = 40
PAIRS = 8
OWN = 30
OWN_STEP = 10
REST_STEP = 12
CELLS = PW * H
LEVELS = 32767.0
f32, bf16 = jnp.float32, jnp.bfloat16


def group_mean(v):
    lane = lax.broadcasted_iota(jnp.int32, v.shape, 1)
    pair = v + pltpu.roll(v, F - 1, 1)
    four = pair + pltpu.roll(pair, F - 2, 1)
    head = jnp.where(lane % 4 == 0, four, 0.0)
    two = head + pltpu.roll(head, 1, 1)
    return 0.25 * (two + pltpu.roll(two, 2, 1))


def merge(stats, count, total, squares):
    number, mean, spread = stats
    total = jnp.broadcast_to(jnp.sum(total, axis=0, keepdims=True), (8, F))
    squares = jnp.broadcast_to(jnp.sum(squares, axis=0, keepdims=True), (8, F))
    number = number + count
    return number, mean + total / number, spread + (squares - total * total / number)


def norm_affine(mean, squares):
    center = group_mean(mean)
    spread = group_mean(squares / CELLS + jnp.square(mean - center))
    rstd = 1.0 / jnp.sqrt(spread + norm_epsilon)
    return rstd, -center * rstd


def silu_of_twice(u):
    return u + u * jnp.tanh(u)


def kernel(
    owners,
    offset_ref,
    count_ref,
    noisy_ref,
    cond_ref,
    w_in_ref,
    w_mid_ref,
    w_out_ref,
    mod_ref,
    out_ref,
    own_x,
    own_k,
    side_x,
    side_k,
    info,
    info_side,
    term_send,
    term_side,
    step_send,
    step_side,
    term_mid,
    arrived,
    blend,
    source,
    stacked,
    ring1,
    ring1b,
    feats,
    sums,
    ring2,
    ring2b,
    rolled,
    terms,
    w1,
    w1b,
    w2,
    w3,
    local_sem,
    send_sem,
    recv_sem,
):
    me, core = lax.axis_index("owner"), lax.axis_index("ens")
    left = lax.rem(me + owners - 1, owners)
    right = lax.rem(me + 1, owners)
    targets = (right, left)

    barrier = pltpu.get_barrier_semaphore()
    for neighbour in (left, right):
        pl.semaphore_signal(barrier, inc=1, device_id=(neighbour, core), device_id_type=MESH)

    local = [
        pltpu.make_async_copy(noisy_ref, own_x, local_sem.at[0]),
        pltpu.make_async_copy(cond_ref, own_k, local_sem.at[1]),
        pltpu.make_async_copy(w_mid_ref, rolled, local_sem.at[2]),
    ]
    for copy in local:
        copy.start()

    def both(kind, make):
        copies = []
        for side in range(2):
            source_ref, target_ref = make(side)
            copies.append(
                pltpu.make_async_remote_copy(
                    src_ref=source_ref,
                    dst_ref=target_ref,
                    send_sem=send_sem.at[kind, side],
                    recv_sem=recv_sem.at[kind, side],
                    device_id=(targets[side], core),
                    device_id_type=MESH,
                )
            )
        return copies

    send_x = [
        both(m, lambda side: (noisy_ref.at[m], side_x.at[side, m])) for m in range(2)
    ]
    send_k = both(2, lambda side: (cond_ref, side_k.at[side]))
    send_info = both(3, lambda side: (info, info_side.at[side]))

    def term_copies(m, part):
        levels = both(
            4 + 2 * m + part,
            lambda side: (term_send.at[side, m, part], term_side.at[side, m, part]),
        )
        steps = both(
            8 + 2 * m + part,
            lambda side: (step_send.at[side, m, part], step_side.at[side, m, part]),
        )
        return levels, steps

    send_term = [[term_copies(m, part) for part in range(2)] for m in range(2)]

    offset, count = offset_ref[0], count_ref[0]
    info[0], info[1] = offset, count
    pl.semaphore_wait(barrier, 2)
    for copy in send_x[0] + send_k + send_info:
        copy.start()

    active = [core * 2 + m < count for m in range(2)]
    odd = offset & 1
    even = offset - odd
    left_pairs = 33 - (offset >> 1)

    taps = w_in_ref[...].astype(f32)
    zeros128 = jnp.zeros((F, F), bf16)
    zeros8, zeros16 = jnp.zeros((8, F), f32), jnp.zeros((16, F), f32)
    for ci in range(4):
        for p in range(2):
            a = ci - p
            block = block_b = zeros128
            if 0 <= a < 3:
                pieces, pieces_b = [], []
                for b in range(3):
                    tap = taps[(a * 3 + b) * 24 : (a * 3 + b) * 24 + 24]
                    pieces += [tap, zeros16]
                    pieces_b += [zeros16[:C], tap[C:], tap[:C], zeros16[:4]]
                block = jnp.concatenate(pieces + [zeros8], axis=0).astype(bf16)
                block_b = jnp.concatenate(pieces_b + [zeros8], axis=0).astype(bf16)
            w1[pl.ds(ci * 128, 128), pl.ds(p * 128, 128)] = block
            w1b[pl.ds(ci * 128, 128), pl.ds(p * 128, 128)] = block_b

    def put_state(ref, slot, block):
        for c in range(C):
            scaled = (input_scale * ref[c].astype(f32)).astype(bf16).astype(f32)
            source[pl.ds((slot + c) * STRIDE + block * BW, BW)] = scaled

    def put_cond(ref, block):
        for c in range(C):
            source[pl.ds((C + c) * STRIDE + block * BW, BW)] = ref[c].astype(f32)

    local[0].wait()
    local[1].wait()
    source[pl.ds(36 * STRIDE, 4 * STRIDE)] = jnp.zeros((4 * STRIDE, H), f32)
    put_cond(own_k, 1)
    put_state(own_x.at[0], 0, 1)
    put_state(own_x.at[1], 24, 1)

    def stack_column(column, channels, valid=None):
        v = source[pl.ds(column, channels, stride=STRIDE), :]
        if valid is not None:
            v = jnp.where(valid, v, 0.0)
        row = lax.broadcasted_iota(jnp.int32, v.shape, 1)
        before = jnp.where(row == 0, 0.0, pltpu.roll(v, 1, 1))
        after = jnp.where(row == H - 1, 0.0, pltpu.roll(v, H - 1, 1))
        pieces = []
        for part in (before, v, after):
            pieces += [part] if channels == LANES else [part, zeros16]
        return jnp.concatenate(pieces + [zeros8], axis=0).T.astype(bf16)

    def own_stack_step(i, carry):
        for t in range(16):
            stacked[t % 2, i * 8 + t // 2] = stack_column(BW + 1 + i * 16 + t, LANES)
        return carry

    lax.fori_loop(0, 4, own_stack_step, 0)

    def deviations(stats, values, keep=None):
        deviation = values.reshape(-1, 8, F) - stats[1]
        if keep is not None:
            deviation = jnp.where(keep, deviation, 0.0)
        return jnp.sum(deviation, axis=0), jnp.sum(deviation * deviation, axis=0)

    def own_conv(m, i, stats):
        columns = []
        for ci in range(4):
            part = stacked[ci % 2, pl.ds(i * OWN_STEP + ci // 2, OWN_STEP)]
            columns.append(part.reshape(OWN_STEP * H, F))
        lhs = jnp.concatenate(columns, axis=1)
        acc = jnp.dot(lhs, (w1, w1b)[m][...], preferred_element_type=f32)
        total = squares = jnp.zeros((8, F), f32)
        for p in range(2):
            half = acc[:, p * F : (p + 1) * F]
            feats[p, pl.ds(m * OWN + i * OWN_STEP, OWN_STEP)] = half.reshape(OWN_STEP, H, F)
            more = deviations(stats, half)
            total, squares = total + more[0], squares + more[1]
        return merge(stats, 2.0 * OWN_STEP * H, total, squares)

    zero = jnp.zeros((8, F), f32)
    own_steps = OWN // OWN_STEP
    own_stats = lax.fori_loop(0, own_steps, functools.partial(own_conv, 0), (zero, zero, zero))

    place = lax.broadcasted_iota(jnp.int32, (PW, H), 0).astype(f32)
    angle = jnp.square((place + 0.5) * (math.pi / PW) - math.pi / 2)
    wave = jnp.zeros((PW, H), f32)
    for n in range(8, -1, -1):
        wave = wave * angle + (-1.0) ** n / math.factorial(2 * n)
    blend[pl.ds(0, BW)] = jnp.zeros((BW, H), f32)
    blend[pl.ds(BW, PW)] = 0.1 + wave * wave
    blend[pl.ds(BW + PW, BW)] = jnp.zeros((BW, H), f32)
    for c in range(C):
        arrived[0, c, pl.ds(BW, BW)] = jnp.zeros((BW, H), f32)
        arrived[1, c, pl.ds(0, BW)] = jnp.zeros((BW, H), f32)

    out_rows = jnp.concatenate([w_out_ref[...].astype(f32), jnp.zeros((4, F), f32)], axis=0)
    spread_rows = jnp.broadcast_to(out_rows[:, None, :], (16, 8, F)).reshape(F, F).T
    lane = lax.broadcasted_iota(jnp.int32, (F, F), 1)
    for k in range(8):
        w3[pl.ds(k * 128, 128)] = jnp.where(lane % 8 == k, spread_rows, 0.0).astype(bf16)
    local[2].wait()
    for b in range(3):
        for ci in range(4):
            for p in range(2):
                a = ci - p
                block = rolled[a * 3 + b] if 0 <= a < 3 else zeros128
                w2[pl.ds((b * 4 + ci) * 128, 128), pl.ds(p * 128, 128)] = block

    rings1 = (ring1, ring1b)
    terms[:, pl.ds(0, BW)] = jnp.zeros((C, BW, H), f32)
    terms[:, pl.ds(BW + PW, BW)] = jnp.zeros((C, BW, H), f32)

    def rest_stack(g):
        for t in range(2 * REST_STEP + 4):
            place = 2 * REST_STEP * g + t
            first_right = 68 - even
            column = jnp.where(place < first_right, even - 1 + place, 125 - first_right + place)
            valid = (column >= offset) & (column < offset + PW)
            column = jnp.clip(column, 0, STRIDE - 1)
            rings1[g % 2][t % 2, t // 2] = stack_column(column, 24, valid)

    def rest_conv(g, m, stats):
        columns = []
        for ci in range(4):
            parts = []
            for p in range(REST_STEP):
                skip = (REST_STEP * g + p >= left_pairs).astype(jnp.int32)
                parts.append(rings1[g % 2][ci % 2, p + ci // 2 + skip])
            columns.append(jnp.concatenate(parts, axis=0))
        lhs = jnp.concatenate(columns, axis=1)
        acc = jnp.dot(lhs, w1[...], preferred_element_type=f32)
        total = squares = jnp.zeros((8, F), f32)
        number = 2.0 * REST_STEP * H
        for p in range(2):
            half = acc[:, p * F : (p + 1) * F]
            feats[p, pl.ds(2 * OWN + g * REST_STEP, REST_STEP)] = half.reshape(REST_STEP, H, F)
            start, stop = 0, REST_STEP * H
            if g == 0 and p == 0:
                start = H
                more = deviations(stats, half[:H], odd == 0)
                total, squares = total + more[0], squares + more[1]
                number = number - odd.astype(f32) * H
            if g == 2:
                stop = (REST_STEP - 2) * H
                if p == 0:
                    more = deviations(stats, half[stop : stop + H], odd == 1)
                    total, squares = total + more[0], squares + more[1]
                    number = number - 4.0 * H + odd.astype(f32) * H
            more = deviations(stats, half[start:stop])
            total, squares = total + more[0], squares + more[1]
        return merge(stats, number, total, squares)

    def first_at(m, column):
        place = offset + column
        pair, parity = place >> 1, place & 1
        rest = 2 * OWN + jnp.where(pair < 33, pair - (offset >> 1), pair - 63 + left_pairs)
        own = m * OWN + pair - 33
        slot = jnp.where((pair >= 33) & (pair < 63), own, rest)
        return feats[parity, slot]

    def put_hidden(m, affine, column, places):
        h = silu_of_twice(first_at(m, jnp.minimum(column, PW - 1)) * affine[0] + affine[1])
        if any(t == 2 * PAIRS + 1 for _, t in places):
            h = jnp.where(column < PW, h, 0.0)
        row = lax.broadcasted_iota(jnp.int32, h.shape, 0)
        before = jnp.where(row == 0, 0.0, pltpu.roll(h, 1, 0))
        after = jnp.where(row == H - 1, 0.0, pltpu.roll(h, H - 1, 0))
        for b, value in enumerate((before, h, after)):
            for ref, t in places:
                ref[b, t % 2, t // 2] = value.astype(bf16)

    def fill(m, affine, g, here, there):
        for r in range(2 * PAIRS):
            places = [(here, r + 2)]
            if r >= 2 * PAIRS - 2:
                places.append((there, r + 2 - 2 * PAIRS))
            put_hidden(m, affine, 2 * PAIRS * g + 1 + r, places)

    def mid_conv(m, g, ref, stats):
        columns = []
        for b in range(3):
            for ci in range(4):
                part = ref[b, ci % 2, pl.ds(ci // 2, PAIRS)]
                columns.append(part.reshape(PAIRS * H, F))
        acc = jnp.dot(jnp.concatenate(columns, axis=1), w2[...], preferred_element_type=f32)
        total = squares = jnp.zeros((8, F), f32)
        for q in range(PAIRS):
            for p in range(2):
                both_convs = acc[q * H : (q + 1) * H, p * F : (p + 1) * F]
                both_convs = both_convs + first_at(m, 2 * (PAIRS * g + q) + p)
                sums[p, PAIRS * g + q] = both_convs
                more = deviations(stats, both_convs)
                total, squares = total + more[0], squares + more[1]
        return merge(stats, 2.0 * PAIRS * H, total, squares)

    def mid_step(i, carry, m):
        stats, affine = carry
        stats = mid_conv(m, 2 * i, ring2, stats)
        fill(m, affine, 2 * i + 1, ring2b, ring2)
        stats = mid_conv(m, 2 * i + 1, ring2b, stats)
        fill(m, affine, 2 * i + 2, ring2, ring2b)
        return stats, affine

    def out_columns(part, affine):
        columns = []
        for k in range(8):
            rows = []
            for g in range(4):
                u = sums[k % 2, part * 16 + g * 4 + k // 2] * affine[0] + affine[1]
                rows.append(silu_of_twice(u).astype(bf16))
            columns.append(jnp.concatenate(rows, axis=0))
        result = jnp.dot(jnp.concatenate(columns, axis=1), w3[...], preferred_element_type=f32)
        for g in range(4):
            flipped = result[g * H : (g + 1) * H].T.reshape(16, 8, H)[:C]
            at = 32 * part + g * 8
            weight = blend[pl.ds(BW + at, 8)] * (-step_factor * output_scale)
            terms[:, pl.ds(BW + at, 8)] = flipped * weight

    routes = ((1, 0), (1, 1), (0, 1), (0, 0))

    def send_columns(part, m):
        side, half = routes[part]
        values = [terms[c, pl.ds(BW + 32 * part, 32)].reshape(4, 8, H) for c in range(C)]
        largest = jnp.full((8, H), 1e-30, f32)
        for value in values:
            largest = jnp.maximum(largest, jnp.max(jnp.abs(value), axis=0))
        step_send[side, m, half] = jnp.where(active[m], largest * (1.0 / LEVELS), 0.0)
        inverse = LEVELS / largest
        for c in range(C):
            levels = jnp.round(values[c] * inverse).astype(jnp.int32)
            term_send[side, m, half, c] = levels.reshape(32, H).astype(jnp.int16)
        for copies in send_term[m][half]:
            copies[side].start()

    def keep_own(m):
        for c in range(C):
            part = terms[c, pl.ds(2 * BW - offset, BW)]
            term_mid[m, c] = jnp.where(active[m], part, 0.0)

    def put_sides(m):
        put_state(side_x.at[0, m], 0, 0)
        put_state(side_x.at[1, m], 0, 2)

    def hidden_affine(stats):
        scale, bias = norm_affine(stats[1], stats[2])
        gain = 1.0 + mod_ref[0:1]
        return (scale * gain * 0.5)[0:1], ((bias * gain + mod_ref[1:2]) * 0.5)[0:1]

    def middle(m, stats):
        affine = hidden_affine(stats)
        for b in range(3):
            ring2[b, 0, 0] = zeros128
        put_hidden(m, affine, jnp.int32(0), [(ring2, 1)])
        fill(m, affine, 0, ring2, ring2b)
        (stats, _) = lax.fori_loop(
            0,
            BW // PAIRS // 2,
            functools.partial(mid_step, m=m),
            ((zero, stats[1], zero), affine),
        )
        scale, bias = norm_affine(stats[1], stats[2])
        return scale[0:1] * 0.5, bias[0:1] * 0.5

    for copy in send_k:
        copy.wait_recv()
    put_cond(side_k.at[0], 0)
    put_cond(side_k.at[1], 2)
    for copy in send_x[0]:
        copy.wait_recv()
    for copy in send_x[1]:
        copy.start()
    put_sides(0)

    stats, other = own_stats, (zero, zero, zero)
    rest_stack(0)
    for g in range(3):
        other = own_conv(1, g, other)
        if g < 2:
            rest_stack(g + 1)
        stats = rest_conv(g, 0, stats)
    affine = middle(0, stats)

    for copy in send_x[1] + send_info:
        copy.wait_recv()
    put_state(own_x.at[1], 0, 1)
    put_sides(1)
    stats = other
    rest_stack(0)
    out_columns(0, affine)
    for g in range(3):
        if g < 2:
            rest_stack(g + 1)
        stats = rest_conv(g, 1, stats)
        out_columns(g + 1, affine)
    for part in range(4):
        send_columns(part, 0)
    keep_own(0)

    affine = middle(1, stats)
    for part in (0, 3, 1, 2):
        out_columns(part, affine)
        send_columns(part, 1)
    keep_own(1)

    shifts = (offset, info_side[0, 0], info_side[1, 0])
    starts = (2 * BW - shifts[0], BW + PW - shifts[1], BW - shifts[2])
    members = (count, info_side[0, 1], info_side[1, 1])
    planes = [blend[pl.ds(start, BW)] for start in starts]
    inverse = 1.0 / (planes[0] + planes[1] + planes[2])
    for m in range(2):
        factor = jnp.zeros((BW, H), f32)
        for plane, number in zip(planes, members):
            factor = factor + jnp.where(core * 2 + m < number, plane, 0.0)
        factor = factor * (step_factor * (1.0 - skip_scale))
        for half in range(2):
            for copies in send_term[m][half]:
                for copy in copies:
                    copy.wait_recv()
            for side in range(2):
                step = step_side[side, m, half]
                at = BW + 32 * half if side == 1 else 32 * (1 - half)
                for c in range(C):
                    levels = term_side[side, m, half, c].astype(jnp.int32).astype(f32)
                    values = (levels.reshape(4, 8, H) * step).reshape(32, H)
                    arrived[side, c, pl.ds(at, 32)] = values
        for c in range(C):
            x = own_x[m, c].astype(f32)
            numerator = term_mid[m, c]
            for side in range(2):
                numerator = numerator + arrived[side, c, pl.ds(BW - shifts[1 + side], BW)]
            out_ref[m, c] = x + (x * factor + numerator) * inverse

    sent = send_k + send_info
    for m in range(2):
        sent = sent + send_x[m]
        for half in range(2):
            for copies in send_term[m][half]:
                sent = sent + copies
    for copy in sent:
        copy.wait_send()


def solution(mesh):
    owners = mesh.shape["owner"]
    def on_device(noisy, cond, counts, offsets, w_in, w_mid, w_out, mod):
        smem = pl.BlockSpec(memory_space=pltpu.SMEM)
        vmem = pl.BlockSpec(memory_space=pltpu.VMEM)
        hbm = pl.BlockSpec(memory_space=pl.ANY)
        return pl.pallas_call(
            functools.partial(kernel, owners),
            out_shape=jax.ShapeDtypeStruct((2, C, BW, H), f32),
            in_specs=[smem, smem, hbm, hbm, vmem, hbm, vmem, vmem],
            out_specs=vmem,
            scratch_shapes=[
                pltpu.VMEM((2, C, BW, H), bf16),
                pltpu.VMEM((C, BW, H), bf16),
                pltpu.VMEM((2, 2, C, BW, H), bf16),
                pltpu.VMEM((2, C, BW, H), bf16),
                pltpu.SMEM((2,), jnp.int32),
                pltpu.SMEM((2, 2), jnp.int32),
                pltpu.VMEM((2, 2, 2, C, 32, H), jnp.int16),
                pltpu.VMEM((2, 2, 2, C, 32, H), jnp.int16),
                pltpu.VMEM((2, 2, 2, 8, H), f32),
                pltpu.VMEM((2, 2, 2, 8, H), f32),
                pltpu.VMEM((2, C, BW, H), f32),
                pltpu.VMEM((2, C, PW, H), f32),
                pltpu.VMEM((2 * PW, H), f32),
                pltpu.VMEM((LANES * STRIDE, H), f32),
                pltpu.VMEM((2, BW // 2, H, F), bf16),
                pltpu.VMEM((2, REST_STEP + 2, H, F), bf16),
                pltpu.VMEM((2, REST_STEP + 2, H, F), bf16),
                pltpu.VMEM((2, 2 * OWN + 3 * REST_STEP, H, F), f32),
                pltpu.VMEM((2, BW, H, F), f32),
                pltpu.VMEM((3, 2, PAIRS + 1, H, F), bf16),
                pltpu.VMEM((3, 2, PAIRS + 1, H, F), bf16),
                pltpu.VMEM((9, F, F), bf16),
                pltpu.VMEM((C, 2 * PW, H), f32),
                pltpu.VMEM((4 * F, 2 * F), bf16),
                pltpu.VMEM((4 * F, 2 * F), bf16),
                pltpu.VMEM((12 * F, 2 * F), bf16),
                pltpu.VMEM((8 * F, F), bf16),
                pltpu.SemaphoreType.DMA((3,)),
                pltpu.SemaphoreType.DMA((12, 2)),
                pltpu.SemaphoreType.DMA((12, 2)),
            ],
            compiler_params=pltpu.CompilerParams(
                collective_id=0, has_side_effects=True, vmem_limit_bytes=56 * 2**20
            ),
            cost_estimate=pl.CostEstimate(
                flops=24 * 10**9, bytes_accessed=4 * 10**6, transcendentals=8 * 10**6
            ),
        )(
            offsets,
            counts,
            noisy,
            cond,
            w_in.reshape(216, F),
            w_mid.reshape(9, F, F),
            w_out,
            mod,
        )

    placed = (
        P("ens", None, "owner", None),
        P(None, "owner", None),
        P("owner"),
        P("owner"),
        P(),
        P(),
        P(),
        P(),
    )
    return jax.shard_map(
        on_device,
        mesh=mesh,
        in_specs=placed,
        out_specs=P("ens", None, "owner", None),
        check_vma=False,
    )
```

```python
import functools
import math

import jax
import jax.numpy as jnp
from jax import lax
from jax.experimental import pallas as pl
from jax.experimental.pallas import tpu as pltpu
from jax.sharding import PartitionSpec as P

MESH = pl.DeviceIdType.MESH

sigma_now = 2.0
sigma_next = 1.0
sigma_data = 0.5
input_scale = 1.0 / math.sqrt(sigma_now**2 + sigma_data**2)
skip_scale = sigma_data**2 / (sigma_now**2 + sigma_data**2)
output_scale = sigma_now * sigma_data / math.sqrt(sigma_now**2 + sigma_data**2)
step_factor = (sigma_next - sigma_now) / sigma_now
norm_epsilon = 1e-05

C = 12
F = 128
BW = 64
PW = 128
H = 128
STRIDE = 200
LANES = 40
PAIRS = 8
OWN = 30
OWN_STEP = 10
REST_STEP = 12
CELLS = PW * H
LEVELS = 32767.0
f32, bf16 = jnp.float32, jnp.bfloat16


def group_mean(v):
    lane = lax.broadcasted_iota(jnp.int32, v.shape, 1)
    pair = v + pltpu.roll(v, F - 1, 1)
    four = pair + pltpu.roll(pair, F - 2, 1)
    head = jnp.where(lane % 4 == 0, four, 0.0)
    two = head + pltpu.roll(head, 1, 1)
    return 0.25 * (two + pltpu.roll(two, 2, 1))


def merge(stats, count, total, squares):
    number, mean, spread = stats
    total = jnp.broadcast_to(jnp.sum(total, axis=0, keepdims=True), (8, F))
    squares = jnp.broadcast_to(jnp.sum(squares, axis=0, keepdims=True), (8, F))
    number = number + count
    return number, mean + total / number, spread + (squares - total * total / number)


def norm_affine(mean, squares):
    center = group_mean(mean)
    spread = group_mean(squares / CELLS + jnp.square(mean - center))
    rstd = 1.0 / jnp.sqrt(spread + norm_epsilon)
    return rstd, -center * rstd


def silu_of_twice(u):
    return u + u * jnp.tanh(u)


def kernel(
    owners,
    offset_ref,
    count_ref,
    noisy_ref,
    cond_ref,
    w_in_ref,
    w_mid_ref,
    w_out_ref,
    mod_ref,
    out_ref,
    own_x,
    own_k,
    side_x,
    side_k,
    info,
    info_side,
    term_send,
    term_side,
    step_send,
    step_side,
    term_mid,
    arrived,
    blend,
    source,
    stacked,
    ring1,
    ring1b,
    feats,
    sums,
    ring2,
    ring2b,
    rolled,
    terms,
    w1,
    w1b,
    w2,
    w3,
    local_sem,
    send_sem,
    recv_sem,
):
    me, core = lax.axis_index("owner"), lax.axis_index("ens")
    left = lax.rem(me + owners - 1, owners)
    right = lax.rem(me + 1, owners)
    targets = (right, left)

    barrier = pltpu.get_barrier_semaphore()
    for neighbour in (left, right):
        pl.semaphore_signal(barrier, inc=1, device_id=(neighbour, core), device_id_type=MESH)
    pl.semaphore_signal(barrier, inc=1, device_id=(me, 1 - core), device_id_type=MESH)

    local = [
        pltpu.make_async_copy(noisy_ref, own_x, local_sem.at[0]),
        pltpu.make_async_copy(cond_ref, own_k, local_sem.at[1]),
        pltpu.make_async_copy(w_mid_ref, rolled, local_sem.at[2]),
    ]
    for copy in local:
        copy.start()

    def both(kind, make, across=False):
        copies = []
        for side in range(2):
            source_ref, target_ref = make(side)
            copies.append(
                pltpu.make_async_remote_copy(
                    src_ref=source_ref,
                    dst_ref=target_ref,
                    send_sem=send_sem.at[kind, side],
                    recv_sem=recv_sem.at[kind, side],
                    device_id=(me, 1 - core) if across else (targets[side], core),
                    device_id_type=MESH,
                )
            )
        return copies

    send_x = [
        both(m, lambda side: (noisy_ref.at[m], side_x.at[side, m])) for m in range(2)
    ]
    half_k = pl.ds(core * (C // 2), C // 2)
    send_k = both(2, lambda side: (cond_ref.at[half_k], side_k.at[side, half_k]))
    share_k = both(
        12, lambda side: (side_k.at[side, half_k], side_k.at[side, half_k]), across=True
    )
    send_info = both(3, lambda side: (info, info_side.at[side]))

    def term_copies(m, part):
        levels = both(
            4 + 2 * m + part,
            lambda side: (term_send.at[side, m, part], term_side.at[side, m, part]),
        )
        steps = both(
            8 + 2 * m + part,
            lambda side: (step_send.at[side, m, part], step_side.at[side, m, part]),
        )
        return levels, steps

    send_term = [[term_copies(m, part) for part in range(2)] for m in range(2)]

    offset, count = offset_ref[0], count_ref[0]
    info[0], info[1] = offset, count
    pl.semaphore_wait(barrier, 3)
    for copy in send_k + send_x[0] + send_info:
        copy.start()

    active = [core * 2 + m < count for m in range(2)]
    odd = offset & 1
    even = offset - odd
    left_pairs = 33 - (offset >> 1)

    taps = w_in_ref[...].astype(f32)
    zeros128 = jnp.zeros((F, F), bf16)
    zeros8, zeros16 = jnp.zeros((8, F), f32), jnp.zeros((16, F), f32)
    for ci in range(4):
        for p in range(2):
            a = ci - p
            block = block_b = zeros128
            if 0 <= a < 3:
                pieces, pieces_b = [], []
                for b in range(3):
                    tap = taps[(a * 3 + b) * 24 : (a * 3 + b) * 24 + 24]
                    pieces += [tap, zeros16]
                    pieces_b += [zeros16[:C], tap[C:], tap[:C], zeros16[:4]]
                block = jnp.concatenate(pieces + [zeros8], axis=0).astype(bf16)
                block_b = jnp.concatenate(pieces_b + [zeros8], axis=0).astype(bf16)
            w1[pl.ds(ci * 128, 128), pl.ds(p * 128, 128)] = block
            w1b[pl.ds(ci * 128, 128), pl.ds(p * 128, 128)] = block_b

    def put_state(ref, slot, block):
        for c in range(C):
            scaled = (input_scale * ref[c].astype(f32)).astype(bf16).astype(f32)
            source[pl.ds((slot + c) * STRIDE + block * BW, BW)] = scaled

    def put_cond(ref, block):
        for c in range(C):
            source[pl.ds((C + c) * STRIDE + block * BW, BW)] = ref[c].astype(f32)

    local[0].wait()
    local[1].wait()
    source[pl.ds(36 * STRIDE, 4 * STRIDE)] = jnp.zeros((4 * STRIDE, H), f32)
    put_cond(own_k, 1)
    put_state(own_x.at[0], 0, 1)
    put_state(own_x.at[1], 24, 1)

    def stack_column(column, channels, valid=None):
        v = source[pl.ds(column, channels, stride=STRIDE), :]
        if valid is not None:
            v = jnp.where(valid, v, 0.0)
        row = lax.broadcasted_iota(jnp.int32, v.shape, 1)
        before = jnp.where(row == 0, 0.0, pltpu.roll(v, 1, 1))
        after = jnp.where(row == H - 1, 0.0, pltpu.roll(v, H - 1, 1))
        pieces = []
        for part in (before, v, after):
            pieces += [part] if channels == LANES else [part, zeros16]
        return jnp.concatenate(pieces + [zeros8], axis=0).T.astype(bf16)

    def own_stack_step(i, carry):
        for t in range(16):
            stacked[t % 2, i * 8 + t // 2] = stack_column(BW + 1 + i * 16 + t, LANES)
        return carry

    lax.fori_loop(0, 4, own_stack_step, 0)
    for copy, share in zip(send_k, share_k):
        copy.wait_recv()
        share.start()

    def deviations(stats, values, keep=None):
        deviation = values.reshape(-1, 8, F) - stats[1]
        if keep is not None:
            deviation = jnp.where(keep, deviation, 0.0)
        return jnp.sum(deviation, axis=0), jnp.sum(deviation * deviation, axis=0)

    def own_conv(m, i, stats):
        columns = []
        for ci in range(4):
            part = stacked[ci % 2, pl.ds(i * OWN_STEP + ci // 2, OWN_STEP)]
            columns.append(part.reshape(OWN_STEP * H, F))
        lhs = jnp.concatenate(columns, axis=1)
        acc = jnp.dot(lhs, (w1, w1b)[m][...], preferred_element_type=f32)
        total = squares = jnp.zeros((8, F), f32)
        for p in range(2):
            half = acc[:, p * F : (p + 1) * F]
            feats[p, pl.ds(m * OWN + i * OWN_STEP, OWN_STEP)] = half.reshape(OWN_STEP, H, F)
            more = deviations(stats, half)
            total, squares = total + more[0], squares + more[1]
        return merge(stats, 2.0 * OWN_STEP * H, total, squares)

    zero = jnp.zeros((8, F), f32)
    own_steps = OWN // OWN_STEP
    own_stats = lax.fori_loop(0, own_steps, functools.partial(own_conv, 0), (zero, zero, zero))

    place = lax.broadcasted_iota(jnp.int32, (PW, H), 0).astype(f32)
    angle = jnp.square((place + 0.5) * (math.pi / PW) - math.pi / 2)
    wave = jnp.zeros((PW, H), f32)
    for n in range(8, -1, -1):
        wave = wave * angle + (-1.0) ** n / math.factorial(2 * n)
    blend[pl.ds(0, BW)] = jnp.zeros((BW, H), f32)
    blend[pl.ds(BW, PW)] = 0.1 + wave * wave
    blend[pl.ds(BW + PW, BW)] = jnp.zeros((BW, H), f32)
    for c in range(C):
        arrived[0, c, pl.ds(BW, BW)] = jnp.zeros((BW, H), f32)
        arrived[1, c, pl.ds(0, BW)] = jnp.zeros((BW, H), f32)

    out_rows = jnp.concatenate([w_out_ref[...].astype(f32), jnp.zeros((4, F), f32)], axis=0)
    spread_rows = jnp.broadcast_to(out_rows[:, None, :], (16, 8, F)).reshape(F, F).T
    lane = lax.broadcasted_iota(jnp.int32, (F, F), 1)
    for k in range(8):
        w3[pl.ds(k * 128, 128)] = jnp.where(lane % 8 == k, spread_rows, 0.0).astype(bf16)
    local[2].wait()
    for b in range(3):
        for ci in range(4):
            for p in range(2):
                a = ci - p
                block = rolled[a * 3 + b] if 0 <= a < 3 else zeros128
                w2[pl.ds((b * 4 + ci) * 128, 128), pl.ds(p * 128, 128)] = block

    rings1 = (ring1, ring1b)
    terms[:, pl.ds(0, BW)] = jnp.zeros((C, BW, H), f32)
    terms[:, pl.ds(BW + PW, BW)] = jnp.zeros((C, BW, H), f32)

    def rest_stack(g):
        for t in range(2 * REST_STEP + 4):
            place = 2 * REST_STEP * g + t
            first_right = 68 - even
            column = jnp.where(place < first_right, even - 1 + place, 125 - first_right + place)
            valid = (column >= offset) & (column < offset + PW)
            column = jnp.clip(column, 0, STRIDE - 1)
            rings1[g % 2][t % 2, t // 2] = stack_column(column, 24, valid)

    def rest_conv(g, m, stats):
        columns = []
        for ci in range(4):
            parts = []
            for p in range(REST_STEP):
                skip = (REST_STEP * g + p >= left_pairs).astype(jnp.int32)
                parts.append(rings1[g % 2][ci % 2, p + ci // 2 + skip])
            columns.append(jnp.concatenate(parts, axis=0))
        lhs = jnp.concatenate(columns, axis=1)
        acc = jnp.dot(lhs, w1[...], preferred_element_type=f32)
        total = squares = jnp.zeros((8, F), f32)
        number = 2.0 * REST_STEP * H
        for p in range(2):
            half = acc[:, p * F : (p + 1) * F]
            feats[p, pl.ds(2 * OWN + g * REST_STEP, REST_STEP)] = half.reshape(REST_STEP, H, F)
            start, stop = 0, REST_STEP * H
            if g == 0 and p == 0:
                start = H
                more = deviations(stats, half[:H], odd == 0)
                total, squares = total + more[0], squares + more[1]
                number = number - odd.astype(f32) * H
            if g == 2:
                stop = (REST_STEP - 2) * H
                if p == 0:
                    more = deviations(stats, half[stop : stop + H], odd == 1)
                    total, squares = total + more[0], squares + more[1]
                    number = number - 4.0 * H + odd.astype(f32) * H
            more = deviations(stats, half[start:stop])
            total, squares = total + more[0], squares + more[1]
        return merge(stats, number, total, squares)

    def first_at(m, column):
        place = offset + column
        pair, parity = place >> 1, place & 1
        rest = 2 * OWN + jnp.where(pair < 33, pair - (offset >> 1), pair - 63 + left_pairs)
        own = m * OWN + pair - 33
        slot = jnp.where((pair >= 33) & (pair < 63), own, rest)
        return feats[parity, slot]

    def put_hidden(m, affine, column, places):
        h = silu_of_twice(first_at(m, jnp.minimum(column, PW - 1)) * affine[0] + affine[1])
        if any(t == 2 * PAIRS + 1 for _, t in places):
            h = jnp.where(column < PW, h, 0.0)
        row = lax.broadcasted_iota(jnp.int32, h.shape, 0)
        before = jnp.where(row == 0, 0.0, pltpu.roll(h, 1, 0))
        after = jnp.where(row == H - 1, 0.0, pltpu.roll(h, H - 1, 0))
        for b, value in enumerate((before, h, after)):
            for ref, t in places:
                ref[b, t % 2, t // 2] = value.astype(bf16)

    def fill(m, affine, g, here, there):
        for r in range(2 * PAIRS):
            places = [(here, r + 2)]
            if r >= 2 * PAIRS - 2:
                places.append((there, r + 2 - 2 * PAIRS))
            put_hidden(m, affine, 2 * PAIRS * g + 1 + r, places)

    def mid_conv(m, g, ref, stats):
        columns = []
        for b in range(3):
            for ci in range(4):
                part = ref[b, ci % 2, pl.ds(ci // 2, PAIRS)]
                columns.append(part.reshape(PAIRS * H, F))
        acc = jnp.dot(jnp.concatenate(columns, axis=1), w2[...], preferred_element_type=f32)
        total = squares = jnp.zeros((8, F), f32)
        for q in range(PAIRS):
            for p in range(2):
                both_convs = acc[q * H : (q + 1) * H, p * F : (p + 1) * F]
                both_convs = both_convs + first_at(m, 2 * (PAIRS * g + q) + p)
                sums[p, PAIRS * g + q] = both_convs
                more = deviations(stats, both_convs)
                total, squares = total + more[0], squares + more[1]
        return merge(stats, 2.0 * PAIRS * H, total, squares)

    def mid_step(i, carry, m):
        stats, affine = carry
        stats = mid_conv(m, 2 * i, ring2, stats)
        fill(m, affine, 2 * i + 1, ring2b, ring2)
        stats = mid_conv(m, 2 * i + 1, ring2b, stats)
        fill(m, affine, 2 * i + 2, ring2, ring2b)
        return stats, affine

    def out_columns(part, affine):
        columns = []
        for k in range(8):
            rows = []
            for g in range(4):
                u = sums[k % 2, part * 16 + g * 4 + k // 2] * affine[0] + affine[1]
                rows.append(silu_of_twice(u).astype(bf16))
            columns.append(jnp.concatenate(rows, axis=0))
        result = jnp.dot(jnp.concatenate(columns, axis=1), w3[...], preferred_element_type=f32)
        for g in range(4):
            flipped = result[g * H : (g + 1) * H].T.reshape(16, 8, H)[:C]
            at = 32 * part + g * 8
            weight = blend[pl.ds(BW + at, 8)] * (-step_factor * output_scale)
            terms[:, pl.ds(BW + at, 8)] = flipped * weight

    routes = ((1, 0), (1, 1), (0, 1), (0, 0))

    def send_columns(part, m):
        side, half = routes[part]
        values = [terms[c, pl.ds(BW + 32 * part, 32)].reshape(4, 8, H) for c in range(C)]
        largest = jnp.full((8, H), 1e-30, f32)
        for value in values:
            largest = jnp.maximum(largest, jnp.max(jnp.abs(value), axis=0))
        step_send[side, m, half] = jnp.where(active[m], largest * (1.0 / LEVELS), 0.0)
        inverse = LEVELS / largest
        for c in range(C):
            levels = jnp.round(values[c] * inverse).astype(jnp.int32)
            term_send[side, m, half, c] = levels.reshape(32, H).astype(jnp.int16)
        for copies in send_term[m][half]:
            copies[side].start()

    def keep_own(m):
        for c in range(C):
            part = terms[c, pl.ds(2 * BW - offset, BW)]
            term_mid[m, c] = jnp.where(active[m], part, 0.0)

    def put_sides(m):
        put_state(side_x.at[0, m], 0, 0)
        put_state(side_x.at[1, m], 0, 2)

    def hidden_affine(stats):
        scale, bias = norm_affine(stats[1], stats[2])
        gain = 1.0 + mod_ref[0:1]
        return (scale * gain * 0.5)[0:1], ((bias * gain + mod_ref[1:2]) * 0.5)[0:1]

    def middle(m, stats):
        affine = hidden_affine(stats)
        for b in range(3):
            ring2[b, 0, 0] = zeros128
        put_hidden(m, affine, jnp.int32(0), [(ring2, 1)])
        fill(m, affine, 0, ring2, ring2b)
        (stats, _) = lax.fori_loop(
            0,
            BW // PAIRS // 2,
            functools.partial(mid_step, m=m),
            ((zero, stats[1], zero), affine),
        )
        scale, bias = norm_affine(stats[1], stats[2])
        return scale[0:1] * 0.5, bias[0:1] * 0.5

    for copy in share_k:
        copy.wait_recv()
    put_cond(side_k.at[0], 0)
    put_cond(side_k.at[1], 2)
    for copy in send_x[0]:
        copy.wait_recv()
    for copy in send_x[1]:
        copy.start()
    put_sides(0)

    stats, other = own_stats, (zero, zero, zero)
    rest_stack(0)
    for g in range(3):
        other = own_conv(1, g, other)
        if g < 2:
            rest_stack(g + 1)
        stats = rest_conv(g, 0, stats)
    affine = middle(0, stats)

    for copy in send_x[1] + send_info:
        copy.wait_recv()
    put_state(own_x.at[1], 0, 1)
    put_sides(1)
    stats = other
    rest_stack(0)
    out_columns(0, affine)
    for g in range(3):
        if g < 2:
            rest_stack(g + 1)
        stats = rest_conv(g, 1, stats)
        out_columns(g + 1, affine)
    for part in range(4):
        send_columns(part, 0)
    keep_own(0)

    affine = middle(1, stats)
    for part in (0, 3, 1, 2):
        out_columns(part, affine)
        send_columns(part, 1)
    keep_own(1)

    shifts = (offset, info_side[0, 0], info_side[1, 0])
    starts = (2 * BW - shifts[0], BW + PW - shifts[1], BW - shifts[2])
    members = (count, info_side[0, 1], info_side[1, 1])
    planes = [blend[pl.ds(start, BW)] for start in starts]
    inverse = 1.0 / (planes[0] + planes[1] + planes[2])
    for m in range(2):
        factor = jnp.zeros((BW, H), f32)
        for plane, number in zip(planes, members):
            factor = factor + jnp.where(core * 2 + m < number, plane, 0.0)
        factor = factor * (step_factor * (1.0 - skip_scale))
        for half in range(2):
            for copies in send_term[m][half]:
                for copy in copies:
                    copy.wait_recv()
            for side in range(2):
                step = step_side[side, m, half]
                at = BW + 32 * half if side == 1 else 32 * (1 - half)
                for c in range(C):
                    levels = term_side[side, m, half, c].astype(jnp.int32).astype(f32)
                    values = (levels.reshape(4, 8, H) * step).reshape(32, H)
                    arrived[side, c, pl.ds(at, 32)] = values
        for c in range(C):
            x = own_x[m, c].astype(f32)
            numerator = term_mid[m, c]
            for side in range(2):
                numerator = numerator + arrived[side, c, pl.ds(BW - shifts[1 + side], BW)]
            out_ref[m, c] = x + (x * factor + numerator) * inverse

    sent = send_k + share_k + send_info
    for m in range(2):
        sent = sent + send_x[m]
        for half in range(2):
            for copies in send_term[m][half]:
                sent = sent + copies
    for copy in sent:
        copy.wait_send()


def solution(mesh):
    owners = mesh.shape["owner"]
    def on_device(noisy, cond, counts, offsets, w_in, w_mid, w_out, mod):
        smem = pl.BlockSpec(memory_space=pltpu.SMEM)
        vmem = pl.BlockSpec(memory_space=pltpu.VMEM)
        hbm = pl.BlockSpec(memory_space=pl.ANY)
        return pl.pallas_call(
            functools.partial(kernel, owners),
            out_shape=jax.ShapeDtypeStruct((2, C, BW, H), f32),
            in_specs=[smem, smem, hbm, hbm, vmem, hbm, vmem, vmem],
            out_specs=vmem,
            scratch_shapes=[
                pltpu.VMEM((2, C, BW, H), bf16),
                pltpu.VMEM((C, BW, H), bf16),
                pltpu.VMEM((2, 2, C, BW, H), bf16),
                pltpu.VMEM((2, C, BW, H), bf16),
                pltpu.SMEM((2,), jnp.int32),
                pltpu.SMEM((2, 2), jnp.int32),
                pltpu.VMEM((2, 2, 2, C, 32, H), jnp.int16),
                pltpu.VMEM((2, 2, 2, C, 32, H), jnp.int16),
                pltpu.VMEM((2, 2, 2, 8, H), f32),
                pltpu.VMEM((2, 2, 2, 8, H), f32),
                pltpu.VMEM((2, C, BW, H), f32),
                pltpu.VMEM((2, C, PW, H), f32),
                pltpu.VMEM((2 * PW, H), f32),
                pltpu.VMEM((LANES * STRIDE, H), f32),
                pltpu.VMEM((2, BW // 2, H, F), bf16),
                pltpu.VMEM((2, REST_STEP + 2, H, F), bf16),
                pltpu.VMEM((2, REST_STEP + 2, H, F), bf16),
                pltpu.VMEM((2, 2 * OWN + 3 * REST_STEP, H, F), f32),
                pltpu.VMEM((2, BW, H, F), f32),
                pltpu.VMEM((3, 2, PAIRS + 1, H, F), bf16),
                pltpu.VMEM((3, 2, PAIRS + 1, H, F), bf16),
                pltpu.VMEM((9, F, F), bf16),
                pltpu.VMEM((C, 2 * PW, H), f32),
                pltpu.VMEM((4 * F, 2 * F), bf16),
                pltpu.VMEM((4 * F, 2 * F), bf16),
                pltpu.VMEM((12 * F, 2 * F), bf16),
                pltpu.VMEM((8 * F, F), bf16),
                pltpu.SemaphoreType.DMA((3,)),
                pltpu.SemaphoreType.DMA((13, 2)),
                pltpu.SemaphoreType.DMA((13, 2)),
            ],
            compiler_params=pltpu.CompilerParams(
                collective_id=0, has_side_effects=True, vmem_limit_bytes=56 * 2**20
            ),
            cost_estimate=pl.CostEstimate(
                flops=24 * 10**9, bytes_accessed=4 * 10**6, transcendentals=8 * 10**6
            ),
        )(
            offsets,
            counts,
            noisy,
            cond,
            w_in.reshape(216, F),
            w_mid.reshape(9, F, F),
            w_out,
            mod,
        )

    placed = (
        P("ens", None, "owner", None),
        P(None, "owner", None),
        P("owner"),
        P("owner"),
        P(),
        P(),
        P(),
        P(),
    )
    return jax.shard_map(
        on_device,
        mesh=mesh,
        in_specs=placed,
        out_specs=P("ens", None, "owner", None),
        check_vma=False,
    )
```
